512 devices in a mesh: band: 32 (over y, z_lo, core), ga: 16 (over z_hi, x).
Axes of the slice: x: 4, y: 4, z: 16 (z_hi: 4, z_lo: 4; z = z_hi * 4 + z_lo), core: 2. Of those that a mesh axis runs over, the one named last changes fastest.
Arguments:
- coefficients: bfloat16 [2, 64, 4096, 128], P(None, 'band', 'ga'), may hold values from -6 to 6
- panel: bfloat16 [2, 64, 4096, 128], P(None, 'band', 'ga'), may hold values from -6 to 6
- potential: float32 [128, 128, 128], P('ga'), may hold values from -6 to 6
- stick_columns: int32 [4096], replicated, may hold values from 0 to 16383, as said below
Outputs:
- applied: bfloat16 [2, 64, 4096, 128], P(None, 'band', 'ga')
- intersection: float32 [2, 64, 64], P(None, 'band', 'ga')
The draws below stay inside these ranges and needn't reach their ends.
Inputs may be any that keep to these rules, and one draw needn't show every extreme that they name: `stick_columns`: 4096 distinct grid columns, in ascending order.
All inputs are finite; a program needn't handle non-finite values.
Results may differ from the reference program's by a relative error of at most 0.014.
Values may be sent and summed in bfloat16 or wider, within the bound.
A program may use at most 128 MiB of HBM per device.

```python
import math
import jax
import jax.numpy as jnp
from jax import lax

NX = 128
NY = 128
NZ = 128
STICKS = 4096
BANDS = 64
PANEL = 64


def draw_stick_columns(key, part):
    key = jax.random.fold_in(key, 7)
    columns_all = NX * NY
    interior = jax.random.permutation(key, columns_all - 2)[:STICKS - 2].astype(jnp.int32) + 1
    chosen = jnp.concatenate([jnp.zeros((1,), jnp.int32), interior, jnp.full((1,), columns_all - 1, jnp.int32)])
    return jnp.sort(chosen)


def block_levels(own_key, dims, cuts, low, largest):
    level, own = 1.0, jax.random.fold_in(own_key, 6)
    for axis_at, blocks in cuts:
        steps = jnp.exp(jax.random.uniform(jax.random.fold_in(own, axis_at), (blocks,), jnp.float32, low / len(cuts), largest / len(cuts)))
        level = level * jnp.repeat(steps, dims[axis_at] // blocks).reshape([-1 if axis == axis_at else 1 for axis in range(len(dims))])
    return level


def bell_draw(rng, dims, scale, most, pieces=(), kind=jnp.bfloat16):
    values = jax.random.normal(rng, dims, jnp.float32) * scale
    if len(pieces) > 0:
        values = block_levels(rng, dims, pieces, -0.22, 0.18) * values
    return jnp.clip(values, min=-most, max=most).astype(kind)


def setup_inputs(seed: int = 0) -> dict:
    streams_of = jax.random.split(jax.random.key(seed), 5)
    return {
        "coefficients": bell_draw(streams_of[0], (2, BANDS, STICKS, NZ), 1.0, 6.0, ((1, 32), (2, 16))),
        "panel": bell_draw(streams_of[1], (2, PANEL, STICKS, NZ), 1.0, 6.0, ((1, 32), (2, 16))),
        "potential": bell_draw(streams_of[2], (NZ, NX, NY), 1.0, 6.0, ((0, 16),), jnp.float32),
        "stick_columns": draw_stick_columns(jax.random.fold_in(streams_of[4], 71), 0),
    }


def section_tables(length, orient):
    counter = jnp.arange(length, dtype=jnp.int32)
    phases = (counter[:, None] * counter[None, :]) % length
    angles = phases.astype(jnp.float32) * (2.0 * math.pi / length)
    cosine = jnp.cos(angles)
    sine = jnp.sin(angles) * orient
    from_real = jnp.stack([cosine, sine], axis=1)
    from_imag = jnp.stack([-sine, cosine], axis=1)
    table = jnp.stack([from_real, from_imag]).astype(jnp.bfloat16)
    table = lax.optimization_barrier(table)
    return table.astype(jnp.float32)


def reference(coefficients, panel, potential, stick_columns):
    columns_all = NX * NY
    spread = (STICKS * NZ) ** -0.5
    grid_scale = (NX * NY * NZ) ** -0.5
    ztable_in = section_tables(NZ, 1.0)
    ytable_in = section_tables(NY, 1.0)
    xtable_in = section_tables(NX, 1.0)
    ztable_out = section_tables(NZ, -1.0)
    ytable_out = section_tables(NY, -1.0)
    xtable_out = section_tables(NX, -1.0)
    pot_xyz = jnp.transpose(potential, (1, 2, 0))

    def one_band(band_pair):
        sticks = (jnp.einsum("csk,ckez->esz", band_pair.astype(jnp.float32), ztable_in) * spread).astype(jnp.bfloat16)
        grid = jnp.zeros((2, columns_all, NZ), jnp.bfloat16).at[:, stick_columns].set(sticks).reshape(2, NX, NY, NZ)
        section = jnp.einsum("cxyz,cyek->exkz", grid.astype(jnp.float32), ytable_in).astype(jnp.bfloat16)
        product = (jnp.einsum("cxyz,cxek->ekyz", section.astype(jnp.float32), xtable_in) * pot_xyz).astype(jnp.bfloat16)
        section = jnp.einsum("cxyz,cyek->exkz", product.astype(jnp.float32), ytable_out).astype(jnp.bfloat16)
        final = jnp.einsum("cxyz,cxek->ekyz", section.astype(jnp.float32), xtable_out) * grid_scale
        picked = final.reshape(2, columns_all, NZ)[:, stick_columns].astype(jnp.bfloat16)
        return jnp.einsum("csz,czek->esk", picked.astype(jnp.float32), ztable_out).astype(jnp.bfloat16)

    results = lax.map(one_band, jnp.transpose(coefficients, (1, 0, 2, 3)))
    applied = jnp.transpose(results, (1, 0, 2, 3))
    panel_real = panel[0].reshape(PANEL, STICKS * NZ)
    panel_imag = panel[1].reshape(PANEL, STICKS * NZ)
    block_real = applied[0].reshape(BANDS, STICKS * NZ)
    block_imag = applied[1].reshape(BANDS, STICKS * NZ)
    over_real = jnp.dot(panel_real, block_real.T, preferred_element_type=jnp.float32) + jnp.dot(panel_imag, block_imag.T, preferred_element_type=jnp.float32)
    over_imag = jnp.dot(panel_real, block_imag.T, preferred_element_type=jnp.float32) - jnp.dot(panel_imag, block_real.T, preferred_element_type=jnp.float32)
    intersection = jnp.stack([over_real, over_imag]) * spread
    return applied, intersection
```

```python
import functools
import math

import jax
import jax.numpy as jnp
import ml_dtypes
import numpy as np
from jax import lax
from jax.experimental import pallas as pl
from jax.experimental.pallas import tpu as pltpu
from jax.sharding import PartitionSpec as P

MESH = pl.DeviceIdType.MESH
F32 = jnp.float32
BF16 = jnp.bfloat16
L = 128


def section_table():
    counter = np.arange(L)
    angles = (counter[:, None] * counter[None, :] % L).astype(np.float32)
    angles = angles * np.float32(2.0 * math.pi / L)
    cosine, sine = np.cos(angles), np.sin(angles)
    return np.block([[cosine, sine], [-sine, cosine]])


def dot(left, right, over_left=1, over_right=0):
    numbers = (((over_left,), (over_right,)), ((), ()))
    return lax.dot_general(left, right, numbers, preferred_element_type=F32)


def lanes(parts):
    return jnp.concatenate(parts, axis=1)


def rows(parts):
    return jnp.concatenate(parts, axis=0)


def block(value, row, column):
    return value[row * L : (row + 1) * L, column * L : (column + 1) * L]


def one_hot(condition):
    return jnp.where(condition, 1.0, 0.0).astype(BF16)


def iota(shape, axis):
    return lax.broadcasted_iota(jnp.int32, shape, axis)


def all_to_all(axis, size, me, source, target, send_sem, recv_sem):
    for step in range(1, size):
        peer = lax.rem(me + step, size)
        pltpu.make_async_remote_copy(
            src_ref=source(peer),
            dst_ref=target(me),
            send_sem=send_sem,
            recv_sem=recv_sem,
            device_id={axis: peer},
            device_id_type=MESH,
        ).start()


def wait_all(ref, sem):
    pltpu.make_async_copy(ref, ref, sem).wait()


def kernel(
    nband, nga, spread, grid_scale,
    coeff, panel, pot, cols, tables, applied, inter,
    send1, recv1, send2, recv2, sendp, recvp, send3, recv3,
    flat, flat2, flatp, flat3, senda, recva, sendb, recvb,
    s1, r1, s2, r2, sp, rp, s3, r3, sa, ra, sb, rb,
):
    me_band = lax.axis_index("band")
    me_ga = lax.axis_index("ga")
    barrier = pltpu.get_barrier_semaphore()
    for step in range(1, nga):
        peer = lax.rem(me_ga + step, nga)
        pl.semaphore_signal(barrier, inc=1, device_id={"ga": peer}, device_id_type=MESH)
    for step in range(1, nband):
        peer = lax.rem(me_band + step, nband)
        pl.semaphore_signal(barrier, inc=1, device_id={"band": peer}, device_id_type=MESH)

    inverse, forward, along_z = tables[0], tables[1], tables[2]

    def z_in(band):
        own = lanes([coeff[0, band], coeff[1, band]])
        value = (dot(along_z, own, 1, 1) * spread).astype(BF16)
        for half in range(2):
            send1[band, :, half] = value[:, half * L : (half + 1) * L].reshape(nga, 16, L)

    z_in(0)
    pl.semaphore_wait(barrier, nga + nband - 2)

    def send_sticks(band):
        all_to_all(
            "ga", nga, me_ga,
            lambda peer: send1.at[band, peer], lambda me: recv1.at[band, me],
            s1.at[band], r1.at[band],
        )
        recv1[band, me_ga] = send1[band, me_ga]

    send_sticks(0)
    z_in(1)
    send_sticks(1)

    def pack(real, imag):
        return jnp.concatenate(
            [real.reshape(nband, 8, L), imag.reshape(nband, 8, L)], axis=1
        ).astype(BF16)

    for band in range(2):
        sendp[:, band] = pack(panel[0, band].astype(F32), panel[1, band].astype(F32))
    all_to_all(
        "band", nband, me_band,
        lambda peer: sendp.at[peer], lambda me: recvp.at[me], sp, rp,
    )
    recvp[me_band] = sendp[me_band]

    col_x = lax.shift_right_logical(cols[...], 7)
    col_y = jnp.bitwise_and(cols[...], L - 1)
    blocks = col_x.shape[0]
    sub = iota((L, L), 0)
    lane = iota((L, L), 1)
    hot_x = lanes([one_hot(sub == col_x[t : t + 1, :]) for t in range(blocks)])
    hot_y = lanes([one_hot(sub == col_y[t : t + 1, :]) for t in range(blocks)])
    there = dot(hot_x, hot_y, 1, 1).astype(BF16)
    before = one_hot(sub < lane)
    ones = jnp.ones((L, L), BF16)
    rank = dot(there, before)
    below = dot(one_hot(lane < sub), there).astype(BF16)
    start = dot(below, ones).astype(jnp.int32)
    slot = start + rank.astype(jnp.int32)
    from_lane = jnp.bitwise_and(slot, L - 1)
    present = there.astype(F32) > 0.5
    first = lax.shift_right_logical(start, 7)
    lane_first = lane >= jnp.bitwise_and(start, L - 1)
    expand = rows([one_hot(first == lane), one_hot(first + 1 == lane)])[:, :blocks]
    where = dot(expand, lanes([col_y, col_x]).astype(F32).astype(BF16))
    sel_y = jnp.where(lane_first, block(where, 0, 0), block(where, 1, 0)).astype(jnp.int32)
    sel_x = jnp.where(lane_first, block(where, 0, 1), block(where, 1, 1)).astype(jnp.int32)
    valid_first = jnp.logical_and(sel_x == sub, lane_first)
    valid_second = jnp.logical_and(sel_x == sub, jnp.logical_not(lane_first))
    count = dot(ones, there, 1, 1).astype(BF16)
    start_row = dot(count, before).astype(jnp.int32)
    first_row = lax.shift_right_logical(start_row, 7)[:blocks, :]
    sub_row = iota((blocks, L), 0)
    collect = lanes([one_hot(first_row == sub_row), one_hot(first_row + 1 == sub_row)])

    def take(value, index):
        return jnp.take_along_axis(value, index, axis=1, mode="promise_in_bounds")

    def real_space(band):
        flat[...] = recv1[band].reshape(blocks * 16, L).astype(F32)
        for pair in range(4):
            level = []
            for layer in (2 * pair, 2 * pair + 1):
                both = lanes(
                    [flat[pl.ds(c * 8 + layer, blocks, stride=16), :] for c in range(2)]
                ).astype(BF16)
                runs = dot(expand, both)
                planes = []
                for c in range(2):
                    run = jnp.where(lane_first, block(runs, 0, c), block(runs, 1, c))
                    planes.append(jnp.where(present, take(run, from_lane), 0.0).astype(BF16))
                level.append(dot(lanes(planes), inverse).astype(BF16))
            turned = rows([lanes([one[:, c * L : (c + 1) * L] for one in level]) for c in range(2)])
            local = lanes([pot[2 * pair], pot[2 * pair + 1]])
            product = (dot(forward, turned) * rows([local, local])).astype(BF16)
            turned = rows([lanes([block(product, e, p) for e in range(2)]) for p in range(2)])
            half = dot(turned, forward).astype(BF16)
            turned = rows([lanes([block(half, p, c) for p in range(2)]) for c in range(2)])
            final = (dot(inverse, turned) * grid_scale).astype(BF16).astype(F32)
            for p in range(2):
                picks = []
                for e in range(2):
                    got = take(block(final, e, p), sel_y)
                    picks.append(
                        rows(
                            [
                                jnp.where(valid_first, got, 0.0).astype(BF16),
                                jnp.where(valid_second, got, 0.0).astype(BF16),
                            ]
                        )
                    )
                sticks = dot(collect, lanes(picks))
                for e in range(2):
                    flat2[pl.ds(e * 8 + 2 * pair + p, blocks, stride=16), :] = sticks[
                        :, e * L : (e + 1) * L
                    ]
        send2[band] = flat2[...].reshape(nga, 2, 16, L).astype(BF16)

    for band in range(2):
        wait_all(recv1.at[band, pl.ds(0, nga - 1)], r1.at[band])
        real_space(band)
        all_to_all(
            "ga", nga, me_ga,
            lambda peer: send2.at[band, peer], lambda me: recv2.at[band, me],
            s2.at[band], r2.at[band],
        )
        recv2[band, me_ga] = send2[band, me_ga]

    wait_all(recvp.at[pl.ds(0, nband - 1)], rp)
    flatp[...] = recvp[...].reshape(nband * 32, L).astype(F32)
    left = lanes(
        [
            rows([flatp[pl.ds(b * 16 + j, nband, stride=32), :] for b in range(2)])
            for j in range(16)
        ]
    ).astype(BF16)

    for band in range(2):
        wait_all(recv2.at[band, pl.ds(0, nga - 1)], r2.at[band])
        own = lanes([recv2[band, :, half].reshape(nga * 16, L) for half in range(2)])
        result = dot(own, along_z, 0, 0)
        for e in range(2):
            applied[e, band] = result[:, e * L : (e + 1) * L].astype(BF16)
        send3[:, band] = pack(result[:, :L], result[:, L:])
        all_to_all(
            "band", nband, me_band,
            lambda peer: send3.at[peer, band], lambda me: recv3.at[me, band],
            s3.at[band], r3.at[band],
        )
        recv3[me_band, band] = send3[me_band, band]
    for band in range(2):
        wait_all(recv3.at[pl.ds(0, nband - 1), band], r3.at[band])

    flat3[...] = recv3[...].reshape(nband * 32, L).astype(F32)
    parts = [flat3[pl.ds(j, nband * 2, stride=16), :].astype(BF16) for j in range(16)]
    right = rows([lanes(parts), lanes(parts[8:] + [-one for one in parts[:8]])])
    value = dot(left, right, 1, 1) * spread
    senda[:, 0, :] = value[:nband]
    senda[:, 1, :] = value[nband:]
    all_to_all(
        "band", nband, me_band,
        lambda peer: senda.at[peer], lambda me: recva.at[me], sa, ra,
    )
    recva[me_band] = senda[me_band]
    wait_all(recva.at[pl.ds(0, nband - 1)], ra)
    sendb[...] = jnp.sum(recva[...], axis=0)
    all_to_all(
        "ga", nga, me_ga,
        lambda peer: sendb, lambda me: recvb.at[me], sb, rb,
    )
    recvb[me_ga] = sendb[...]
    wait_all(recvb.at[pl.ds(0, nga - 1)], rb)
    total = jnp.sum(recvb[...], axis=0)
    total = rows([total, jnp.zeros((6, L), F32)])
    width = inter.shape[2]
    for e in range(2):
        index = jnp.bitwise_and(iota((8, L), 1) + (e * (L // 2) + me_ga * width), L - 1)
        inter[e] = take(total, index)[:2, :width]

    for band in range(2):
        wait_all(send1.at[band, pl.ds(0, nga - 1)], s1.at[band])
        wait_all(send2.at[band, pl.ds(0, nga - 1)], s2.at[band])
        wait_all(send3.at[pl.ds(0, nband - 1), band], s3.at[band])
    wait_all(sendp.at[pl.ds(0, nband - 1)], sp)
    wait_all(senda.at[pl.ds(0, nband - 1)], sa)
    wait_all(recvb.at[pl.ds(0, nga - 1)], sb)


def solution(mesh):
    nband, nga = mesh.shape["band"], mesh.shape["ga"]

    def per_device(coefficients, panel, potential, stick_columns):
        sticks = stick_columns.shape[0]
        depth = coefficients.shape[3]
        spread = 1.0 / math.sqrt(sticks * depth)
        grid_scale = 1.0 / math.sqrt(L * L * depth)
        inverse = section_table()
        layers = L // nga
        along_z = inverse.T.reshape(2, nga, layers, 2 * L).transpose(1, 0, 2, 3)
        tables = np.stack([inverse, inverse.T, along_z.reshape(2 * L, 2 * L)])
        vmem = pl.BlockSpec(memory_space=pltpu.VMEM)
        dma = pltpu.SemaphoreType.DMA
        applied, intersection = pl.pallas_call(
            functools.partial(kernel, nband, nga, spread, grid_scale),
            out_shape=(
                jax.ShapeDtypeStruct(coefficients.shape, BF16),
                jax.ShapeDtypeStruct((2, 2, 2 * nband // nga), F32),
            ),
            in_specs=[vmem] * 5,
            out_specs=(vmem, vmem),
            scratch_shapes=[
                pltpu.VMEM((2, nga, 2, 16, L), BF16),
                pltpu.VMEM((2, nga, 2, 16, L), BF16),
                pltpu.VMEM((2, nga, 2, 16, L), BF16),
                pltpu.VMEM((2, nga, 2, 16, L), BF16),
                pltpu.VMEM((nband, 2, 16, L), BF16),
                pltpu.VMEM((nband, 2, 16, L), BF16),
                pltpu.VMEM((nband, 2, 16, L), BF16),
                pltpu.VMEM((nband, 2, 16, L), BF16),
                pltpu.VMEM((nga * 32, L), F32),
                pltpu.VMEM((nga * 32, L), F32),
                pltpu.VMEM((nband * 32, L), F32),
                pltpu.VMEM((nband * 32, L), F32),
                pltpu.VMEM((nband, 2, L), F32),
                pltpu.VMEM((nband, 2, L), F32),
                pltpu.VMEM((2, L), F32),
                pltpu.VMEM((nga, 2, L), F32),
                dma((2,)), dma((2,)), dma((2,)), dma((2,)), dma, dma,
                dma((2,)), dma((2,)), dma, dma, dma, dma,
            ],
            compiler_params=pltpu.CompilerParams(
                collective_id=0, has_side_effects=True, vmem_limit_bytes=48 * 2**20
            ),
        )(
            coefficients,
            panel,
            potential,
            stick_columns.reshape(sticks // L, L),
            jnp.asarray(tables.astype(ml_dtypes.bfloat16)),
        )
        return applied, intersection

    in_specs = (P(None, "band", "ga", None), P(None, "band", "ga", None), P("ga", None, None), P())
    out_specs = (P(None, "band", "ga", None), P(None, "band", "ga"))
    return jax.shard_map(
        per_device, mesh=mesh, in_specs=in_specs, out_specs=out_specs, check_vma=False
    )
```

```python
import functools
import math

import jax
import jax.numpy as jnp
import ml_dtypes
import numpy as np
from jax import lax
from jax.experimental import pallas as pl
from jax.experimental.pallas import tpu as pltpu
from jax.sharding import PartitionSpec as P

MESH = pl.DeviceIdType.MESH
F32 = jnp.float32
BF16 = jnp.bfloat16
L = 128


def section_table():
    counter = np.arange(L)
    angles = (counter[:, None] * counter[None, :] % L).astype(np.float32)
    angles = angles * np.float32(2.0 * math.pi / L)
    cosine, sine = np.cos(angles), np.sin(angles)
    return np.block([[cosine, sine], [-sine, cosine]])


def dot(left, right, over_left=1, over_right=0):
    numbers = (((over_left,), (over_right,)), ((), ()))
    return lax.dot_general(left, right, numbers, preferred_element_type=F32)


def lanes(parts):
    return jnp.concatenate(parts, axis=1)


def rows(parts):
    return jnp.concatenate(parts, axis=0)


def block(value, row, column):
    return value[row * L : (row + 1) * L, column * L : (column + 1) * L]


def one_hot(condition):
    return jnp.where(condition, 1.0, 0.0).astype(BF16)


def iota(shape, axis):
    return lax.broadcasted_iota(jnp.int32, shape, axis)


def order(axis, size):
    if axis != "ga":
        return list(range(1, size))
    return [(z, x) for z in (2, 1, 3, 0) for x in range(4) if z or x]


def all_to_all(axis, size, me, source, target, send_sem, recv_sem):
    for step in order(axis, size):
        if isinstance(step, tuple):
            peer = lax.rem(me // 4 + step[0], 4) * 4 + lax.rem(lax.rem(me, 4) + step[1], 4)
        else:
            peer = lax.rem(me + step, size)
        pltpu.make_async_remote_copy(
            src_ref=source(peer),
            dst_ref=target(me),
            send_sem=send_sem,
            recv_sem=recv_sem,
            device_id={axis: peer},
            device_id_type=MESH,
        ).start()


def wait_all(ref, sem):
    pltpu.make_async_copy(ref, ref, sem).wait()


def kernel(
    nband, nga, spread, grid_scale,
    coeff_hbm, panel_hbm, pot_hbm, cols_hbm, tables_hbm, applied, inter,
    coeff, panel, pot, cols, cols_s, tables, first_v, first_s, window, place,
    send1, recv1, send2, recv2, sendp, recvp, recv3,
    flat, grid, picked, stage, flatp, flat3, senda, recva, sendb, recvb,
    load, s1, r1, s2, r2, sp, rp, s3, r3, sa, ra, sb, rb,
):
    loads = [
        pltpu.make_async_copy(source, target, load.at[i])
        for i, (source, target) in enumerate(
            [
                (coeff_hbm, coeff),
                (tables_hbm, tables),
                (cols_hbm, cols),
                (cols_hbm, cols_s),
                (panel_hbm, panel),
                (pot_hbm, pot),
            ]
        )
    ]
    for copy in loads:
        copy.start()
    me_band = lax.axis_index("band")
    me_ga = lax.axis_index("ga")
    barrier = pltpu.get_barrier_semaphore()
    for step in range(1, nga):
        peer = lax.rem(me_ga + step, nga)
        pl.semaphore_signal(barrier, inc=1, device_id={"ga": peer}, device_id_type=MESH)
    for step in range(1, nband):
        peer = lax.rem(me_band + step, nband)
        pl.semaphore_signal(barrier, inc=1, device_id={"band": peer}, device_id_type=MESH)

    loads[0].wait()
    loads[1].wait()
    inverse, forward = tables[0], tables[1]

    def z_section(source, band):
        value = dot(tables[2], lanes([source[0, band], source[1, band]]), 1, 1)
        return [value[:, t * L : (t + 1) * L].reshape(nga * 2, 8, L) for t in range(2)]

    def tiles(parts):
        return jnp.concatenate(parts, axis=1).astype(BF16)

    def z_in(band):
        send1[band] = tiles([one * spread for one in z_section(coeff, band)])

    z_in(0)
    pl.semaphore_wait(barrier, nga + nband - 2)

    def send_sticks(band):
        for half in range(2):
            all_to_all(
                "ga", nga, me_ga,
                lambda peer: send1.at[band, peer * 2 + half], lambda me: recv1.at[band, half, me],
                s1.at[band, half], r1.at[band, half],
            )
            recv1[band, half, me_ga] = send1[band, me_ga * 2 + half]

    send_sticks(0)
    z_in(1)
    send_sticks(1)

    loads[4].wait()
    for band in range(2):
        sendp[:, band] = tiles(z_section(panel, band))
    all_to_all(
        "band", nband, me_band,
        lambda peer: sendp.at[peer], lambda me: recvp.at[me], sp, rp,
    )
    recvp[me_band] = sendp[me_band]

    loads[2].wait()
    loads[3].wait()
    col_x = lax.shift_right_logical(cols[...], 7)
    col_y = jnp.bitwise_and(cols[...], L - 1)
    blocks = col_x.shape[0]
    sub = iota((L, L), 0)
    lane = iota((L, L), 1)
    hot_x = lanes([one_hot(sub == col_x[t : t + 1, :]) for t in range(blocks)])
    hot_y = lanes([one_hot(sub == col_y[t : t + 1, :]) for t in range(blocks)])
    there = dot(hot_x, hot_y, 1, 1).astype(BF16)
    before = one_hot(sub < lane)
    ones = jnp.ones((L, L), BF16)
    rank = dot(there, before)
    below = dot(one_hot(lane < sub), there).astype(BF16)
    start = dot(below, ones).astype(jnp.int32)
    slot = start + rank.astype(jnp.int32)
    from_lane = jnp.bitwise_and(slot, L - 1)
    present = there.astype(F32) > 0.5
    first = lax.shift_right_logical(start, 7)
    lane_first = lane >= jnp.bitwise_and(start, L - 1)
    window[...] = jnp.where(lane_first, 1, 0)
    expand = rows([one_hot(first == lane), one_hot(first + 1 == lane)])[:, :blocks]
    where = dot(expand, lanes([col_y, col_x]).astype(F32).astype(BF16))
    sel_y = jnp.where(lane_first, block(where, 0, 0), block(where, 1, 0)).astype(jnp.int32)
    sel_x = jnp.where(lane_first, block(where, 0, 1), block(where, 1, 1)).astype(jnp.int32)
    place[...] = jnp.where(sel_x == sub, jnp.where(lane_first, 1, 2), 0)
    count = dot(ones, there, 1, 1).astype(BF16)
    start_row = dot(count, before)[:8].astype(jnp.int32)
    first_v[...] = jnp.minimum(lax.shift_right_logical(start_row, 7), blocks)
    to_scalars = pltpu.make_async_copy(first_v, first_s, load.at[6])
    to_scalars.start()
    flat[blocks:] = jnp.zeros((2, 8, L), F32)
    to_scalars.wait()

    def take(value, index):
        return jnp.take_along_axis(value, index, axis=1, mode="promise_in_bounds")

    def real_space(band, half):
        flat[:blocks] = recv1[band, half].astype(F32).reshape(blocks, 8, L)
        for x in range(L):
            at = first_s[0, x]
            grid[x * 8 : (x + 1) * 8, :] = jnp.where(
                window[x : x + 1, :] == 1, flat[at], flat[at + 1]
            )
        for pair in range(2):
            level = []
            for layer in (2 * pair, 2 * pair + 1):
                planes = []
                for c in range(2):
                    run = grid[pl.ds(c * 4 + layer, L, stride=8), :]
                    planes.append(jnp.where(present, take(run, from_lane), 0.0).astype(BF16))
                level.append(dot(lanes(planes), inverse).astype(BF16))
            turned = rows([lanes([one[:, c * L : (c + 1) * L] for one in level]) for c in range(2)])
            local = lanes([pot[4 * half + 2 * pair], pot[4 * half + 2 * pair + 1]])
            product = (dot(forward, turned) * rows([local, local])).astype(BF16)
            turned = rows([lanes([block(product, e, p) for e in range(2)]) for p in range(2)])
            level = dot(turned, forward).astype(BF16)
            turned = rows([lanes([block(level, p, c) for p in range(2)]) for c in range(2)])
            final = dot(inverse, turned) * grid_scale
            for p in range(2):
                for e in range(2):
                    picked[pl.ds(e * 4 + 2 * pair + p, L, stride=8), :] = take(
                        block(final, e, p), sel_y
                    )
        held = jnp.zeros((8, L), F32)
        for x in range(L):
            row = picked[x * 8 : (x + 1) * 8, :]
            part = place[x : x + 1, :]
            held = jnp.where(part == 1, row, held)
            stage[x] = held
            held = jnp.where(part == 2, row, held)
        for peer in range(nga):
            both = [
                stage[lax.shift_right_logical(cols_s[t, L - 1], 7)] for t in (2 * peer, 2 * peer + 1)
            ]
            send2[band, half, peer] = rows(both).astype(BF16)

    loads[5].wait()
    chunks = [(band, half) for band in range(2) for half in range(2)]
    for band, half in chunks:
        wait_all(recv1.at[band, half, pl.ds(0, nga - 1)], r1.at[band, half])
        real_space(band, half)
        all_to_all(
            "ga", nga, me_ga,
            lambda peer: send2.at[band, half, peer], lambda me: recv2.at[band, half, me],
            s2.at[band, half], r2.at[band, half],
        )
        recv2[band, half, me_ga] = send2[band, half, me_ga]

    order_j = [t * 8 + e * 4 + layer for e in range(2) for t in range(2) for layer in range(4)]
    wait_all(recvp.at[pl.ds(0, nband - 1)], rp)
    flatp[...] = recvp[...].reshape(nband * 32, L).astype(F32)
    left = lanes(
        [
            rows([flatp[pl.ds(b * 16 + j, nband, stride=32), :] for b in range(2)])
            for j in order_j
        ]
    ).astype(BF16)

    def forward_copy(band, half, member):
        target = member * 2 + half
        return pltpu.make_async_remote_copy(
            src_ref=recv2.at[band, half, member],
            dst_ref=recv3.at[me_band, band],
            send_sem=s3.at[band],
            recv_sem=r3.at[band],
            device_id={"band": target},
            device_id_type=MESH,
        )

    for band, half in chunks:
        wait_all(recv2.at[band, half, pl.ds(0, nga - 1)], r2.at[band, half])
        mine = lax.rem(me_band, 2) == half
        for step in range(1, nga):
            forward_copy(band, half, lax.rem(me_band // 2 + step, nga)).start()

        @pl.when(jnp.logical_not(mine))
        def _():
            forward_copy(band, half, me_band // 2).start()

        @pl.when(mine)
        def _():
            recv3[me_band, band] = recv2[band, half, me_band // 2]

    for band in range(2):
        own = rows(
            [
                lanes([recv2[band, half].astype(F32)[:, t * 8 : t * 8 + 8].reshape(L, L) for t in range(2)])
                for half in range(2)
            ]
        ).astype(BF16)
        result = dot(own, tables[3], 0, 0).astype(BF16)
        for e in range(2):
            applied[e, band] = result[:, e * L : (e + 1) * L]
    for band in range(2):
        wait_all(recv3.at[pl.ds(0, nband - 1), band], r3.at[band])

    flat3[...] = recv3[...].reshape(nband * 32, L).astype(F32)
    parts = [flat3[pl.ds(j, nband * 2, stride=16), :].astype(BF16) for j in order_j]
    right = rows([lanes(parts), lanes(parts[8:] + [-one for one in parts[:8]])])
    value = dot(left, right, 1, 1) * spread
    senda[:, 0, :] = value[:nband]
    senda[:, 1, :] = value[nband:]
    all_to_all(
        "band", nband, me_band,
        lambda peer: senda.at[peer], lambda me: recva.at[me], sa, ra,
    )
    recva[me_band] = senda[me_band]
    wait_all(recva.at[pl.ds(0, nband - 1)], ra)
    sendb[...] = jnp.sum(recva[...], axis=0)
    all_to_all(
        "ga", nga, me_ga,
        lambda peer: sendb, lambda me: recvb.at[me], sb, rb,
    )
    recvb[me_ga] = sendb[...]
    wait_all(recvb.at[pl.ds(0, nga - 1)], rb)
    total = jnp.sum(recvb[...], axis=0)
    total = rows([total, jnp.zeros((6, L), F32)])
    width = inter.shape[2]
    for e in range(2):
        index = jnp.bitwise_and(iota((8, L), 1) + (e * (L // 2) + me_ga * width), L - 1)
        inter[e] = take(total, index)[:2, :width]

    for band in range(2):
        for half in range(2):
            wait_all(send1.at[band, pl.ds(0, nga - 1)], s1.at[band, half])
            wait_all(send2.at[band, half, pl.ds(0, nga - 1)], s2.at[band, half])
        wait_all(recv3.at[pl.ds(0, nband - 1), band], s3.at[band])
    wait_all(sendp.at[pl.ds(0, nband - 1)], sp)
    wait_all(senda.at[pl.ds(0, nband - 1)], sa)
    wait_all(recvb.at[pl.ds(0, nga - 1)], sb)


def solution(mesh):
    nband, nga = mesh.shape["band"], mesh.shape["ga"]

    def per_device(coefficients, panel, potential, stick_columns):
        sticks = stick_columns.shape[0]
        depth = coefficients.shape[3]
        spread = 1.0 / math.sqrt(sticks * depth)
        grid_scale = 1.0 / math.sqrt(L * L * depth)
        inverse = section_table()
        split = inverse.T.reshape(2, nga, 2, 4, 2 * L)
        orders = [split.transpose(1, 2, 0, 3, 4), split.transpose(2, 1, 0, 3, 4)]
        tables = np.stack([inverse, inverse.T] + [one.reshape(2 * L, 2 * L) for one in orders])
        vmem = pl.BlockSpec(memory_space=pltpu.VMEM)
        hbm = pl.BlockSpec(memory_space=pl.ANY)
        blocks = sticks // L
        dma = pltpu.SemaphoreType.DMA
        applied, intersection = pl.pallas_call(
            functools.partial(kernel, nband, nga, spread, grid_scale),
            out_shape=(
                jax.ShapeDtypeStruct(coefficients.shape, BF16),
                jax.ShapeDtypeStruct((2, 2, 2 * nband // nga), F32),
            ),
            in_specs=[hbm] * 5,
            out_specs=(vmem, vmem),
            scratch_shapes=[
                pltpu.VMEM(coefficients.shape, BF16),
                pltpu.VMEM(panel.shape, BF16),
                pltpu.VMEM(potential.shape, F32),
                pltpu.VMEM((blocks, L), jnp.int32),
                pltpu.SMEM((blocks, L), jnp.int32),
                pltpu.VMEM(tables.shape, BF16),
                pltpu.VMEM((8, L), jnp.int32),
                pltpu.SMEM((8, L), jnp.int32),
                pltpu.VMEM((L, L), jnp.int32),
                pltpu.VMEM((L, L), jnp.int32),
                pltpu.VMEM((2, nga * 2, 16, L), BF16),
                pltpu.VMEM((2, 2, nga, 16, L), BF16),
                pltpu.VMEM((2, 2, nga, 16, L), BF16),
                pltpu.VMEM((2, 2, nga, 16, L), BF16),
                pltpu.VMEM((nband, 2, 16, L), BF16),
                pltpu.VMEM((nband, 2, 16, L), BF16),
                pltpu.VMEM((nband, 2, 16, L), BF16),
                pltpu.VMEM((blocks + 2, 8, L), F32),
                pltpu.VMEM((L * 8, L), F32),
                pltpu.VMEM((L * 8, L), F32),
                pltpu.VMEM((L, 8, L), F32),
                pltpu.VMEM((nband * 32, L), F32),
                pltpu.VMEM((nband * 32, L), F32),
                pltpu.VMEM((nband, 2, L), F32),
                pltpu.VMEM((nband, 2, L), F32),
                pltpu.VMEM((2, L), F32),
                pltpu.VMEM((nga, 2, L), F32),
                dma((7,)), dma((2, 2)), dma((2, 2)), dma((2, 2)), dma((2, 2)), dma, dma,
                dma((2,)), dma((2,)), dma, dma, dma, dma,
            ],
            compiler_params=pltpu.CompilerParams(
                collective_id=0, has_side_effects=True, vmem_limit_bytes=63 * 2**20
            ),
        )(
            coefficients,
            panel,
            potential,
            stick_columns.reshape(sticks // L, L),
            jnp.asarray(tables.astype(ml_dtypes.bfloat16)),
        )
        return applied, intersection

    in_specs = (P(None, "band", "ga", None), P(None, "band", "ga", None), P("ga", None, None), P())
    out_specs = (P(None, "band", "ga", None), P(None, "band", "ga"))
    return jax.shard_map(
        per_device, mesh=mesh, in_specs=in_specs, out_specs=out_specs, check_vma=False
    )
```

```python
import functools
import math

import jax
import jax.numpy as jnp
import ml_dtypes
import numpy as np
from jax import lax
from jax.experimental import pallas as pl
from jax.experimental.pallas import tpu as pltpu
from jax.sharding import PartitionSpec as P

MESH = pl.DeviceIdType.MESH
F32 = jnp.float32
BF16 = jnp.bfloat16
L = 128


def section_table():
    counter = np.arange(L)
    angles = (counter[:, None] * counter[None, :] % L).astype(np.float32)
    angles = angles * np.float32(2.0 * math.pi / L)
    cosine, sine = np.cos(angles), np.sin(angles)
    return np.block([[cosine, sine], [-sine, cosine]])


def dot(left, right, over_left=1, over_right=0):
    numbers = (((over_left,), (over_right,)), ((), ()))
    return lax.dot_general(left, right, numbers, preferred_element_type=F32)


def lanes(parts):
    return jnp.concatenate(parts, axis=1)


def rows(parts):
    return jnp.concatenate(parts, axis=0)


def block(value, row, column):
    return value[row * L : (row + 1) * L, column * L : (column + 1) * L]


def one_hot(condition):
    return jnp.where(condition, 1.0, 0.0).astype(BF16)


def iota(shape, axis):
    return lax.broadcasted_iota(jnp.int32, shape, axis)


def wait_all(ref, sem):
    pltpu.make_async_copy(ref, ref, sem).wait()


class Place:
    def __init__(self, nband, nga):
        self.band, self.ga = lax.axis_index("band"), lax.axis_index("ga")
        self.low = self.band // 2 % 4
        self.line = self.low * nga + self.ga
        self.side = self.band // 8 * 2 + self.band % 2
        along = [8, 7, 9, 6, 10, 5, 11, 4, 12, 3, 13, 2, 14, 1, 15, 0]
        self.steps = [(z, x) for z in along for x in range(4) if z or x]

    def line_peer(self, step):
        z = lax.rem(self.ga // 4 * 4 + self.low + step[0], 16)
        return lax.rem(z, 4), z // 4 * 4 + lax.rem(lax.rem(self.ga, 4) + step[1], 4)

    def line_id(self, low, ga):
        return {"band": self.band // 8 * 8 + low * 2 + lax.rem(self.band, 2), "ga": ga}

    def side_peer(self, step):
        return lax.rem(self.side + step, 8)

    def side_id(self, side):
        return {"band": side // 2 * 8 + self.low * 2 + lax.rem(side, 2), "ga": self.ga}


def send(source, target, send_sem, recv_sem, device):
    pltpu.make_async_remote_copy(
        src_ref=source,
        dst_ref=target,
        send_sem=send_sem,
        recv_sem=recv_sem,
        device_id=device,
        device_id_type=MESH,
    ).start()


def kernel(
    nband, nga, spread, grid_scale,
    coeff_hbm, panel_hbm, pot_hbm, cols_hbm, tables_hbm, along_hbm, applied, inter,
    coeff, panel, pot, cols, cols_s, tables, along_z, first_v, first_s, window, place,
    send1, recv1, send2, recv2, sendp, linep, recvp, recv3,
    flat, grid, picked, stage, flatp, flat3, senda, recva, sendb, recvb,
    load, s1, r1, s2, r2, sp, rp, sq, rq, s3, r3, sa, ra, sb, rb,
):
    loads = [
        pltpu.make_async_copy(source, target, load.at[i])
        for i, (source, target) in enumerate(
            [
                (coeff_hbm, coeff),
                (along_hbm, along_z),
                (cols_hbm, cols),
                (cols_hbm, cols_s),
                (panel_hbm, panel),
                (pot_hbm, pot),
                (tables_hbm, tables),
            ]
        )
    ]
    for copy in loads:
        copy.start()
    me = Place(nband, nga)
    count_line, count_side = 4 * nga, nband // 4
    barrier = pltpu.get_barrier_semaphore()
    for step in me.steps:
        device = me.line_id(*me.line_peer(step))
        pl.semaphore_signal(barrier, inc=1, device_id=device, device_id_type=MESH)
    for step in range(1, count_side):
        device = me.side_id(me.side_peer(step))
        pl.semaphore_signal(barrier, inc=1, device_id=device, device_id_type=MESH)

    def z_section(source, scale):
        own = lanes([source[part, band] for band in range(2) for part in range(2)])
        value = dot(along_z[...], own, 1, 1)
        if scale is not None:
            value = value * scale
        halves = [value[:, t * L : (t + 1) * L].reshape(count_line, 8, L) for t in range(2)]
        return jnp.concatenate(halves, axis=1).astype(BF16)

    loads[0].wait()
    loads[1].wait()
    send1[...] = z_section(coeff, spread)
    pl.semaphore_wait(barrier, count_line + count_side - 2)

    def to_slabs(source, target, send_sem, recv_sem):
        for step in me.steps:
            low, ga = me.line_peer(step)
            send(
                source.at[low * nga + ga], target.at[me.low, me.ga],
                send_sem, recv_sem.at[me.low], me.line_id(low, ga),
            )
        pltpu.make_async_copy(
            source.at[me.line], target.at[me.low, me.ga], recv_sem.at[me.low]
        ).start()

    to_slabs(send1, recv1, s1, r1)
    loads[4].wait()
    sendp[...] = z_section(panel, None)
    to_slabs(sendp, linep, sp, rp)

    loads[2].wait()
    loads[3].wait()
    col_x = lax.shift_right_logical(cols[...], 7)
    col_y = jnp.bitwise_and(cols[...], L - 1)
    blocks = col_x.shape[0]
    sub = iota((L, L), 0)
    lane = iota((L, L), 1)
    hot_x = lanes([one_hot(sub == col_x[t : t + 1, :]) for t in range(blocks)])
    hot_y = lanes([one_hot(sub == col_y[t : t + 1, :]) for t in range(blocks)])
    there = dot(hot_x, hot_y, 1, 1).astype(BF16)
    before = one_hot(sub < lane)
    ones = jnp.ones((L, L), BF16)
    rank = dot(there, before)
    below = dot(one_hot(lane < sub), there).astype(BF16)
    start = dot(below, ones).astype(jnp.int32)
    slot = start + rank.astype(jnp.int32)
    from_lane = jnp.bitwise_and(slot, L - 1)
    present = there.astype(F32) > 0.5
    first = lax.shift_right_logical(start, 7)
    lane_first = lane >= jnp.bitwise_and(start, L - 1)
    window[...] = jnp.where(lane_first, 1, 0)
    expand = rows([one_hot(first == lane), one_hot(first + 1 == lane)])[:, :blocks]
    where = dot(expand, lanes([col_y, col_x]).astype(F32).astype(BF16))
    sel_y = jnp.where(lane_first, block(where, 0, 0), block(where, 1, 0)).astype(jnp.int32)
    sel_x = jnp.where(lane_first, block(where, 0, 1), block(where, 1, 1)).astype(jnp.int32)
    place[...] = jnp.where(sel_x == sub, jnp.where(lane_first, 1, 2), 0)
    count = dot(ones, there, 1, 1).astype(BF16)
    start_row = dot(count, before)[:8].astype(jnp.int32)
    first_v[...] = jnp.minimum(lax.shift_right_logical(start_row, 7), blocks)
    to_scalars = pltpu.make_async_copy(first_v, first_s, load.at[7])
    to_scalars.start()
    flat[blocks:] = jnp.zeros((2, 8, L), F32)
    to_scalars.wait()

    def take(value, index):
        return jnp.take_along_axis(value, index, axis=1, mode="promise_in_bounds")

    def real_space(chunk):
        flat[:blocks] = recv1[chunk].astype(F32).reshape(blocks, 8, L)
        for x in range(L):
            at = first_s[0, x]
            grid[x * 8 : (x + 1) * 8, :] = jnp.where(
                window[x : x + 1, :] == 1, flat[at], flat[at + 1]
            )
        for pair in range(2):
            level = []
            for layer in range(2):
                planes = []
                for c in range(2):
                    run = grid[pl.ds(pair * 4 + c * 2 + layer, L, stride=8), :]
                    planes.append(jnp.where(present, take(run, from_lane), 0.0).astype(BF16))
                level.append(dot(lanes(planes), inverse).astype(BF16))
            turned = rows([lanes([one[:, c * L : (c + 1) * L] for one in level]) for c in range(2)])
            product = (dot(forward, turned) * rows([local, local])).astype(BF16)
            turned = rows([lanes([block(product, e, p) for e in range(2)]) for p in range(2)])
            level = dot(turned, forward).astype(BF16)
            turned = rows([lanes([block(level, p, c) for p in range(2)]) for c in range(2)])
            final = dot(inverse, turned) * grid_scale
            for p in range(2):
                for e in range(2):
                    picked[pl.ds(pair * 4 + e * 2 + p, L, stride=8), :] = take(
                        block(final, e, p), sel_y
                    )
        held = jnp.zeros((8, L), F32)
        for x in range(L):
            row = picked[x * 8 : (x + 1) * 8, :]
            part = place[x : x + 1, :]
            held = jnp.where(part == 1, row, held)
            stage[x] = held
            held = jnp.where(part == 2, row, held)
        for peer in range(nga):
            both = [
                stage[lax.shift_right_logical(cols_s[t, L - 1], 7)] for t in (2 * peer, 2 * peer + 1)
            ]
            send2[chunk, peer] = rows(both).astype(BF16)

    loads[5].wait()
    loads[6].wait()
    inverse, forward = tables[0], tables[1]
    local = lanes([pot[me.low * 2], pot[me.low * 2 + 1]])
    order_low = [2, 1, 3, 0]

    def send_picked(chunk):
        for step in range(1, count_side):
            side = me.side_peer(step)
            send(
                send2.at[chunk, pl.ds(side * 2, 2)], recv3.at[me.side, chunk],
                s3, r3, me.side_id(side),
            )
        pltpu.make_async_copy(
            send2.at[chunk, pl.ds(me.side * 2, 2)], recv3.at[me.side, chunk], r3
        ).start()

    def send_back(step_low):
        chunk = lax.rem(me.low + step_low, 4)
        for step in (2, 1, 3, 0):
            for x in range(4):
                ga = lax.rem(me.ga // 4 + step, 4) * 4 + lax.rem(lax.rem(me.ga, 4) + x, 4)
                if step_low or step or x:
                    send(send2.at[chunk, ga], recv2.at[me.line], s2, r2, me.line_id(chunk, ga))
                else:
                    pltpu.make_async_copy(send2.at[chunk, ga], recv2.at[me.line], r2).start()

    for step_low in order_low:
        chunk = lax.rem(me.low + step_low, 4)
        wait_all(recv1.at[chunk], r1.at[chunk])
        real_space(chunk)
        send_picked(chunk)

    for low in range(4):
        wait_all(linep.at[low], rp.at[low])
    for step in range(1, count_side):
        side = me.side_peer(step)
        send(linep.at[:, pl.ds(side * 2, 2)], recvp.at[me.side], sq, rq, me.side_id(side))
    pltpu.make_async_copy(linep.at[:, pl.ds(me.side * 2, 2)], recvp.at[me.side], rq).start()
    for step_low in order_low:
        send_back(step_low)

    def gram_rows(wide, part):
        taken = []
        for share in range(2):
            for t in range(2):
                for layer in range(2):
                    at = [share * 16 + t * 8 + b * 4 + part * 2 + layer for b in range(2)]
                    taken.append(rows([wide[pl.ds(one, nband, stride=32), :] for one in at]))
        return lanes(taken).astype(BF16)

    wait_all(recv3, r3)
    flat3[...] = recv3[...].astype(F32).reshape(nband * 32, L)
    right = [gram_rows(flat3, part) for part in range(2)]
    right = rows([lanes(right), lanes([right[1], -right[0]])])
    wait_all(recvp, rq)
    flatp[...] = recvp[...].astype(F32).reshape(nband * 32, L)
    left = lanes([gram_rows(flatp, part) for part in range(2)])
    value = dot(left, right, 1, 1) * spread
    for side in range(8):
        for b in range(2):
            senda[side, b * 4 : b * 4 + 4] = value[b * nband + side * 4 : b * nband + side * 4 + 4]
    for step in range(1, count_side):
        side = me.side_peer(step)
        send(senda.at[side], recva.at[me.side], sa, ra, me.side_id(side))
    recva[me.side] = senda[me.side]
    wait_all(recva.at[pl.ds(0, count_side - 1)], ra)
    summed = jnp.sum(recva[...], axis=0)
    for low in range(4):
        for b in range(2):
            sendb[low, b : b + 1] = summed[b * 4 + low : b * 4 + low + 1]
    for step in me.steps:
        low, ga = me.line_peer(step)
        send(sendb.at[low], recvb.at[me.line], sb, rb, me.line_id(low, ga))
    recvb[me.line] = sendb[me.low]

    wait_all(recv2, r2)
    got = recv2[...].astype(F32)
    own = lanes([got[:, t * 8 : t * 8 + 8].reshape(8 * count_line, L) for t in range(2)])
    result = dot(own.astype(BF16), along_z[...], 0, 0).astype(BF16)
    for band in range(2):
        for e in range(2):
            at = (band * 2 + e) * L
            applied[e, band] = result[:, at : at + L]

    wait_all(recvb.at[pl.ds(0, count_line - 1)], rb)
    total = rows([jnp.sum(recvb[...], axis=0), jnp.zeros((6, L), F32)])
    column = iota((8, L), 1)
    width = inter.shape[2]
    base = me.ga // 4 * 8 + lax.rem(me.ga, 4)
    for e in range(2):
        index = e * (L // 2) + base + lax.rem(column, 2) * 32 + lax.rem(column // 2, 2) * 4
        inter[e] = take(total, index)[:2, :width]

    wait_all(send1.at[pl.ds(0, count_line - 1)], s1)
    wait_all(send1.at[pl.ds(0, count_line - 1)], sp)
    wait_all(send1.at[pl.ds(0, count_line - 1)], s2)
    wait_all(recv3.at[pl.ds(0, count_side - 1)], s3)
    wait_all(recvp.at[pl.ds(0, count_side - 1)], sq)
    wait_all(senda.at[pl.ds(0, count_side - 1)], sa)
    wait_all(recvb.at[pl.ds(0, count_line - 1)], sb)


def solution(mesh):
    nband, nga = mesh.shape["band"], mesh.shape["ga"]

    def per_device(coefficients, panel, potential, stick_columns):
        sticks = stick_columns.shape[0]
        depth = coefficients.shape[3]
        blocks = sticks // L
        line, side = 4 * nga, nband // 4
        spread = 1.0 / math.sqrt(sticks * depth)
        grid_scale = 1.0 / math.sqrt(L * L * depth)
        inverse = section_table()
        tables = np.stack([inverse, inverse.T])
        split = inverse.T.reshape(2, nga, 4, 2, 2 * L).transpose(2, 1, 0, 3, 4)
        along = np.zeros((4, nga, 2, 2, 2, 2, 2 * L))
        for band in range(2):
            along[:, :, band, :, :, band] = split
        along = along.reshape(8 * line, 4 * L)
        vmem = pl.BlockSpec(memory_space=pltpu.VMEM)
        hbm = pl.BlockSpec(memory_space=pl.ANY)
        dma = pltpu.SemaphoreType.DMA
        line_tiles = pltpu.VMEM((line, 16, L), BF16)
        slab_tiles = pltpu.VMEM((4, nga, 16, L), BF16)
        side_tiles = pltpu.VMEM((side, 4, 2, 16, L), BF16)
        applied, intersection = pl.pallas_call(
            functools.partial(kernel, nband, nga, spread, grid_scale),
            out_shape=(
                jax.ShapeDtypeStruct(coefficients.shape, BF16),
                jax.ShapeDtypeStruct((2, 2, 2 * nband // nga), F32),
            ),
            in_specs=[hbm] * 6,
            out_specs=(vmem, vmem),
            scratch_shapes=[
                pltpu.VMEM(coefficients.shape, BF16),
                pltpu.VMEM(panel.shape, BF16),
                pltpu.VMEM(potential.shape, F32),
                pltpu.VMEM((blocks, L), jnp.int32),
                pltpu.SMEM((blocks, L), jnp.int32),
                pltpu.VMEM(tables.shape, BF16),
                pltpu.VMEM(along.shape, BF16),
                pltpu.VMEM((8, L), jnp.int32),
                pltpu.SMEM((8, L), jnp.int32),
                pltpu.VMEM((L, L), jnp.int32),
                pltpu.VMEM((L, L), jnp.int32),
                line_tiles, slab_tiles, slab_tiles, line_tiles,
                line_tiles, slab_tiles, side_tiles, side_tiles,
                pltpu.VMEM((blocks + 2, 8, L), F32),
                pltpu.VMEM((L * 8, L), F32),
                pltpu.VMEM((L * 8, L), F32),
                pltpu.VMEM((L, 8, L), F32),
                pltpu.VMEM((nband * 32, L), F32),
                pltpu.VMEM((nband * 32, L), F32),
                pltpu.VMEM((side, 8, L), F32),
                pltpu.VMEM((side, 8, L), F32),
                pltpu.VMEM((4, 2, L), F32),
                pltpu.VMEM((line, 2, L), F32),
                dma((8,)), dma, dma((4,)), dma, dma, dma, dma((4,)), dma, dma,
                dma, dma, dma, dma, dma, dma,
            ],
            compiler_params=pltpu.CompilerParams(
                collective_id=0, has_side_effects=True, vmem_limit_bytes=int(53.55 * 2**20)
            ),
        )(
            coefficients,
            panel,
            potential,
            stick_columns.reshape(blocks, L),
            jnp.asarray(tables.astype(ml_dtypes.bfloat16)),
            jnp.asarray(along.astype(ml_dtypes.bfloat16)),
        )
        return applied, intersection

    in_specs = (P(None, "band", "ga", None), P(None, "band", "ga", None), P("ga", None, None), P())
    out_specs = (P(None, "band", "ga", None), P(None, "band", "ga"))
    return jax.shard_map(
        per_device, mesh=mesh, in_specs=in_specs, out_specs=out_specs, check_vma=False
    )
```

```python
import functools
import math

import jax
import jax.numpy as jnp
import ml_dtypes
import numpy as np
from jax import lax
from jax.experimental import pallas as pl
from jax.experimental.pallas import tpu as pltpu
from jax.sharding import PartitionSpec as P

MESH = pl.DeviceIdType.MESH
F32 = jnp.float32
BF16 = jnp.bfloat16
L = 128


def section_table():
    counter = np.arange(L)
    angles = (counter[:, None] * counter[None, :] % L).astype(np.float32)
    angles = angles * np.float32(2.0 * math.pi / L)
    cosine, sine = np.cos(angles), np.sin(angles)
    return np.block([[cosine, sine], [-sine, cosine]])


def dot(left, right, over_left=1, over_right=0):
    numbers = (((over_left,), (over_right,)), ((), ()))
    return lax.dot_general(left, right, numbers, preferred_element_type=F32)


def lanes(parts):
    return jnp.concatenate(parts, axis=1)


def rows(parts):
    return jnp.concatenate(parts, axis=0)


def block(value, row, column):
    return value[row * L : (row + 1) * L, column * L : (column + 1) * L]


def one_hot(condition):
    return jnp.where(condition, 1.0, 0.0).astype(BF16)


def iota(shape, axis):
    return lax.broadcasted_iota(jnp.int32, shape, axis)


def wait_all(ref, sem):
    pltpu.make_async_copy(ref, ref, sem).wait()


class Place:
    def __init__(self, nband, nga):
        self.band, self.ga = lax.axis_index("band"), lax.axis_index("ga")
        self.low = self.band // 2 % 4
        self.line = self.low * nga + self.ga
        self.side = self.band // 8 * 2 + self.band % 2
        along = [8, 7, 9, 6, 10, 5, 11, 4, 12, 3, 13, 2, 14, 1, 15, 0]
        self.steps = [(z, x) for z in along for x in range(4) if z or x]

    def line_peer(self, step):
        z = lax.rem(self.ga // 4 * 4 + self.low + step[0], 16)
        return lax.rem(z, 4), z // 4 * 4 + lax.rem(lax.rem(self.ga, 4) + step[1], 4)

    def line_id(self, low, ga):
        return {"band": self.band // 8 * 8 + low * 2 + lax.rem(self.band, 2), "ga": ga}

    def side_peer(self, step):
        return lax.rem(self.side + step, 8)

    def side_id(self, side):
        return {"band": side // 2 * 8 + self.low * 2 + lax.rem(side, 2), "ga": self.ga}


def send(source, target, send_sem, recv_sem, device):
    pltpu.make_async_remote_copy(
        src_ref=source,
        dst_ref=target,
        send_sem=send_sem,
        recv_sem=recv_sem,
        device_id=device,
        device_id_type=MESH,
    ).start()


def kernel(
    nband, nga, spread, grid_scale,
    coeff_hbm, panel_hbm, pot_hbm, cols_hbm, tables_hbm, along_hbm, applied, inter,
    coeff, panel, pot, cols, cols_s, tables, along_z, first_v, first_s, window, place,
    send1, recv1, send2, recv2, sendp, linep, recvp, recv3,
    flat, grid, picked, stage, flatp, flat3, senda, recva, sendb, recvb,
    load, s1, r1, s2, r2, sp, rp, sq, rq, s3, r3, sa, ra, sb, rb,
):
    loads = [
        pltpu.make_async_copy(source, target, load.at[i])
        for i, (source, target) in enumerate(
            [
                (coeff_hbm, coeff),
                (along_hbm, along_z),
                (cols_hbm, cols),
                (cols_hbm, cols_s),
                (panel_hbm, panel),
                (pot_hbm, pot),
                (tables_hbm, tables),
            ]
        )
    ]
    for copy in loads:
        copy.start()
    me = Place(nband, nga)
    count_line, count_side = 4 * nga, nband // 4
    barrier = pltpu.get_barrier_semaphore()
    for step in me.steps:
        device = me.line_id(*me.line_peer(step))
        pl.semaphore_signal(barrier, inc=1, device_id=device, device_id_type=MESH)
    for step in range(1, count_side):
        device = me.side_id(me.side_peer(step))
        pl.semaphore_signal(barrier, inc=1, device_id=device, device_id_type=MESH)

    def z_section(source, scale):
        own = lanes([source[part, band] for band in range(2) for part in range(2)])
        value = dot(along_z[...], own, 1, 1)
        if scale is not None:
            value = value * scale
        halves = [value[:, t * L : (t + 1) * L].reshape(count_line, 8, L) for t in range(2)]
        return jnp.concatenate(halves, axis=1).astype(BF16)

    loads[0].wait()
    loads[1].wait()
    send1[...] = z_section(coeff, spread)
    pl.semaphore_wait(barrier, count_line + count_side - 2)

    def to_slabs(source, target, send_sem, recv_sem):
        for step in me.steps:
            low, ga = me.line_peer(step)
            send(
                source.at[low * nga + ga], target.at[me.low, me.ga],
                send_sem, recv_sem.at[me.low], me.line_id(low, ga),
            )
        pltpu.make_async_copy(
            source.at[me.line], target.at[me.low, me.ga], recv_sem.at[me.low]
        ).start()

    to_slabs(send1, recv1, s1, r1)
    loads[4].wait()
    sendp[...] = z_section(panel, None)
    to_slabs(sendp, linep, sp, rp)

    loads[2].wait()
    loads[3].wait()
    col_x = lax.shift_right_logical(cols[...], 7)
    col_y = jnp.bitwise_and(cols[...], L - 1)
    blocks = col_x.shape[0]
    sub = iota((L, L), 0)
    lane = iota((L, L), 1)
    hot_x = lanes([one_hot(sub == col_x[t : t + 1, :]) for t in range(blocks)])
    hot_y = lanes([one_hot(sub == col_y[t : t + 1, :]) for t in range(blocks)])
    there = dot(hot_x, hot_y, 1, 1).astype(BF16)
    before = one_hot(sub < lane)
    ones = jnp.ones((L, L), BF16)
    rank = dot(there, before)
    below = dot(one_hot(lane < sub), there).astype(BF16)
    start = dot(below, ones).astype(jnp.int32)
    slot = start + rank.astype(jnp.int32)
    from_lane = jnp.bitwise_and(slot, L - 1)
    present = there.astype(F32) > 0.5
    first = lax.shift_right_logical(start, 7)
    lane_first = lane >= jnp.bitwise_and(start, L - 1)
    window[...] = jnp.where(lane_first, 1, 0)
    expand = rows([one_hot(first == lane), one_hot(first + 1 == lane)])[:, :blocks]
    where = dot(expand, lanes([col_y, col_x]).astype(F32).astype(BF16))
    sel_y = jnp.where(lane_first, block(where, 0, 0), block(where, 1, 0)).astype(jnp.int32)
    sel_x = jnp.where(lane_first, block(where, 0, 1), block(where, 1, 1)).astype(jnp.int32)
    place[...] = jnp.where(sel_x == sub, jnp.where(lane_first, 1, 2), 0)
    count = dot(ones, there, 1, 1).astype(BF16)
    start_row = dot(count, before)[:8].astype(jnp.int32)
    first_v[...] = jnp.minimum(lax.shift_right_logical(start_row, 7), blocks)
    to_scalars = pltpu.make_async_copy(first_v, first_s, load.at[7])
    to_scalars.start()
    flat[blocks:] = jnp.zeros((2, 8, L), F32)
    to_scalars.wait()

    def take(value, index):
        return jnp.take_along_axis(value, index, axis=1, mode="promise_in_bounds")

    def real_space(chunk):
        flat[:blocks] = recv1[chunk].astype(F32).reshape(blocks, 8, L)
        for x in range(L):
            at = first_s[0, x]
            grid[x * 8 : (x + 1) * 8, :] = jnp.where(
                window[x : x + 1, :] == 1, flat[at], flat[at + 1]
            )
        for pair in range(2):
            level = []
            for layer in range(2):
                planes = []
                for c in range(2):
                    run = grid[pl.ds(pair * 4 + c * 2 + layer, L, stride=8), :]
                    planes.append(jnp.where(present, take(run, from_lane), 0.0).astype(BF16))
                level.append(dot(lanes(planes), inverse).astype(BF16))
            turned = rows([lanes([one[:, c * L : (c + 1) * L] for one in level]) for c in range(2)])
            product = (dot(forward, turned) * rows([local, local])).astype(BF16)
            turned = rows([lanes([block(product, e, p) for e in range(2)]) for p in range(2)])
            level = dot(turned, forward).astype(BF16)
            turned = rows([lanes([block(level, p, c) for p in range(2)]) for c in range(2)])
            final = dot(inverse, turned) * grid_scale
            for p in range(2):
                for e in range(2):
                    picked[pl.ds(pair * 4 + e * 2 + p, L, stride=8), :] = take(
                        block(final, e, p), sel_y
                    )
        held = jnp.zeros((8, L), F32)
        for x in range(L):
            row = picked[x * 8 : (x + 1) * 8, :]
            part = place[x : x + 1, :]
            held = jnp.where(part == 1, row, held)
            stage[x] = held
            held = jnp.where(part == 2, row, held)
        for peer in range(nga):
            both = [
                stage[lax.shift_right_logical(cols_s[t, L - 1], 7)] for t in (2 * peer, 2 * peer + 1)
            ]
            send2[chunk, peer] = rows(both).astype(BF16)

    loads[5].wait()
    loads[6].wait()
    inverse, forward = tables[0], tables[1]
    local = lanes([pot[me.low * 2], pot[me.low * 2 + 1]])
    order_low = [2, 1, 3, 0]

    def send_picked(chunk):
        for step in range(1, count_side):
            side = me.side_peer(step)
            send(
                send2.at[chunk, pl.ds(side * 2, 2)], recv3.at[me.side, chunk],
                s3, r3, me.side_id(side),
            )
        pltpu.make_async_copy(
            send2.at[chunk, pl.ds(me.side * 2, 2)], recv3.at[me.side, chunk], r3
        ).start()

    def send_back(step_low):
        chunk = lax.rem(me.low + step_low, 4)
        for step in (2, 1, 3, 0):
            for x in range(4):
                ga = lax.rem(me.ga // 4 + step, 4) * 4 + lax.rem(lax.rem(me.ga, 4) + x, 4)
                if step_low or step or x:
                    send(send2.at[chunk, ga], recv2.at[me.line], s2, r2, me.line_id(chunk, ga))
                else:
                    pltpu.make_async_copy(send2.at[chunk, ga], recv2.at[me.line], r2).start()

    for step_low in order_low:
        chunk = lax.rem(me.low + step_low, 4)
        wait_all(recv1.at[chunk], r1.at[chunk])
        real_space(chunk)
        send_picked(chunk)

    for low in range(4):
        wait_all(linep.at[low], rp.at[low])
    for step in range(1, count_side):
        side = me.side_peer(step)
        send(linep.at[:, pl.ds(side * 2, 2)], recvp.at[me.side], sq, rq, me.side_id(side))
    pltpu.make_async_copy(linep.at[:, pl.ds(me.side * 2, 2)], recvp.at[me.side], rq).start()
    for step_low in order_low:
        send_back(step_low)

    def gram_rows(wide, part):
        taken = []
        for share in range(2):
            for t in range(2):
                for layer in range(2):
                    at = [share * 16 + t * 8 + b * 4 + part * 2 + layer for b in range(2)]
                    taken.append(rows([wide[pl.ds(one, nband, stride=32), :] for one in at]))
        return lanes(taken).astype(BF16)

    wait_all(recv3, r3)
    flat3[...] = recv3[...].astype(F32).reshape(nband * 32, L)
    right = [gram_rows(flat3, part) for part in range(2)]
    right = rows([lanes(right), lanes([right[1], -right[0]])])
    wait_all(recvp, rq)
    flatp[...] = recvp[...].astype(F32).reshape(nband * 32, L)
    left = lanes([gram_rows(flatp, part) for part in range(2)])
    value = dot(left, right, 1, 1) * spread
    for side in range(8):
        for b in range(2):
            senda[side, b * 4 : b * 4 + 4] = value[b * nband + side * 4 : b * nband + side * 4 + 4]
    for step in range(1, count_side):
        side = me.side_peer(step)
        send(senda.at[side], recva.at[me.side], sa, ra, me.side_id(side))
    recva[me.side] = senda[me.side]
    wait_all(recva.at[pl.ds(0, count_side - 1)], ra)
    summed = jnp.sum(recva[...], axis=0)
    for low in range(4):
        for b in range(2):
            sendb[low, b : b + 1] = summed[b * 4 + low : b * 4 + low + 1]
    for step in me.steps:
        low, ga = me.line_peer(step)
        send(sendb.at[low], recvb.at[me.line], sb, rb, me.line_id(low, ga))
    recvb[me.line] = sendb[me.low]

    wait_all(recv2, r2)
    got = recv2[...].astype(F32)
    own = lanes([got[:, t * 8 : t * 8 + 8].reshape(8 * count_line, L) for t in range(2)])
    result = dot(own.astype(BF16), along_z[...], 0, 0).astype(BF16)
    for band in range(2):
        for e in range(2):
            at = (band * 2 + e) * L
            applied[e, band] = result[:, at : at + L]

    wait_all(recvb.at[pl.ds(0, count_line - 1)], rb)
    total = rows([jnp.sum(recvb[...], axis=0), jnp.zeros((6, L), F32)])
    column = iota((8, L), 1)
    width = inter.shape[2]
    base = me.ga // 4 * 8 + lax.rem(me.ga, 4)
    for e in range(2):
        index = e * (L // 2) + base + lax.rem(column, 2) * 32 + lax.rem(column // 2, 2) * 4
        inter[e] = take(total, index)[:2, :width]

    wait_all(send1.at[pl.ds(0, count_line - 1)], s1)
    wait_all(send1.at[pl.ds(0, count_line - 1)], sp)
    wait_all(send1.at[pl.ds(0, count_line - 1)], s2)
    wait_all(recv3.at[pl.ds(0, count_side - 1)], s3)
    wait_all(recvp.at[pl.ds(0, count_side - 1)], sq)
    wait_all(senda.at[pl.ds(0, count_side - 1)], sa)
    wait_all(recvb.at[pl.ds(0, count_line - 1)], sb)


def solution(mesh):
    nband, nga = mesh.shape["band"], mesh.shape["ga"]

    def per_device(coefficients, panel, potential, stick_columns):
        sticks = stick_columns.shape[0]
        depth = coefficients.shape[3]
        blocks = sticks // L
        line, side = 4 * nga, nband // 4
        spread = 1.0 / math.sqrt(sticks * depth)
        grid_scale = 1.0 / math.sqrt(L * L * depth)
        inverse = section_table()
        tables = np.stack([inverse, inverse.T])
        split = inverse.T.reshape(2, nga, 4, 2, 2 * L).transpose(2, 1, 0, 3, 4)
        along = np.zeros((4, nga, 2, 2, 2, 2, 2 * L))
        for band in range(2):
            along[:, :, band, :, :, band] = split
        along = along.reshape(8 * line, 4 * L)
        vmem = pl.BlockSpec(memory_space=pltpu.VMEM)
        hbm = pl.BlockSpec(memory_space=pl.ANY)
        dma = pltpu.SemaphoreType.DMA
        line_tiles = pltpu.VMEM((line, 16, L), BF16)
        slab_tiles = pltpu.VMEM((4, nga, 16, L), BF16)
        side_tiles = pltpu.VMEM((side, 4, 2, 16, L), BF16)
        applied, intersection = pl.pallas_call(
            functools.partial(kernel, nband, nga, spread, grid_scale),
            out_shape=(
                jax.ShapeDtypeStruct(coefficients.shape, BF16),
                jax.ShapeDtypeStruct((2, 2, 2 * nband // nga), F32),
            ),
            in_specs=[hbm] * 6,
            out_specs=(vmem, vmem),
            scratch_shapes=[
                pltpu.VMEM(coefficients.shape, BF16),
                pltpu.VMEM(panel.shape, BF16),
                pltpu.VMEM(potential.shape, F32),
                pltpu.VMEM((blocks, L), jnp.int32),
                pltpu.SMEM((blocks, L), jnp.int32),
                pltpu.VMEM(tables.shape, BF16),
                pltpu.VMEM(along.shape, BF16),
                pltpu.VMEM((8, L), jnp.int32),
                pltpu.SMEM((8, L), jnp.int32),
                pltpu.VMEM((L, L), jnp.int32),
                pltpu.VMEM((L, L), jnp.int32),
                line_tiles, slab_tiles, slab_tiles, line_tiles,
                line_tiles, slab_tiles, side_tiles, side_tiles,
                pltpu.VMEM((blocks + 2, 8, L), F32),
                pltpu.VMEM((L * 8, L), F32),
                pltpu.VMEM((L * 8, L), F32),
                pltpu.VMEM((L, 8, L), F32),
                pltpu.VMEM((nband * 32, L), F32),
                pltpu.VMEM((nband * 32, L), F32),
                pltpu.VMEM((side, 8, L), F32),
                pltpu.VMEM((side, 8, L), F32),
                pltpu.VMEM((4, 2, L), F32),
                pltpu.VMEM((line, 2, L), F32),
                dma((8,)), dma, dma((4,)), dma, dma, dma, dma((4,)), dma, dma,
                dma, dma, dma, dma, dma, dma,
            ],
            compiler_params=pltpu.CompilerParams(
                collective_id=0, has_side_effects=True, vmem_limit_bytes=48 * 2**20
            ),
        )(
            *[
                pltpu.with_memory_space_constraint(one, pltpu.HBM)
                for one in (
                    coefficients,
                    panel,
                    potential,
                    stick_columns.reshape(blocks, L),
                    jnp.asarray(tables.astype(ml_dtypes.bfloat16)),
                    jnp.asarray(along.astype(ml_dtypes.bfloat16)),
                )
            ]
        )
        return applied, intersection

    in_specs = (P(None, "band", "ga", None), P(None, "band", "ga", None), P("ga", None, None), P())
    out_specs = (P(None, "band", "ga", None), P(None, "band", "ga"))
    return jax.shard_map(
        per_device, mesh=mesh, in_specs=in_specs, out_specs=out_specs, check_vma=False
    )
```

```python
import functools
import math

import jax
import jax.numpy as jnp
import ml_dtypes
import numpy as np
from jax import lax
from jax.experimental import pallas as pl
from jax.experimental.pallas import tpu as pltpu
from jax.sharding import PartitionSpec as P

MESH = pl.DeviceIdType.MESH
F32 = jnp.float32
BF16 = jnp.bfloat16
L = 128


def section_table():
    counter = np.arange(L)
    angles = (counter[:, None] * counter[None, :] % L).astype(np.float32)
    angles = angles * np.float32(2.0 * math.pi / L)
    cosine, sine = np.cos(angles), np.sin(angles)
    return np.block([[cosine, sine], [-sine, cosine]])


def dot(left, right, over_left=1, over_right=0):
    numbers = (((over_left,), (over_right,)), ((), ()))
    return lax.dot_general(left, right, numbers, preferred_element_type=F32)


def lanes(parts):
    return jnp.concatenate(parts, axis=1)


def rows(parts):
    return jnp.concatenate(parts, axis=0)


def block(value, row, column):
    return value[row * L : (row + 1) * L, column * L : (column + 1) * L]


def one_hot(condition):
    return jnp.where(condition, 1.0, 0.0).astype(BF16)


def iota(shape, axis):
    return lax.broadcasted_iota(jnp.int32, shape, axis)


def wait_all(ref, sem):
    pltpu.make_async_copy(ref, ref, sem).wait()


class Place:
    def __init__(self, nband, nga):
        self.band, self.ga = lax.axis_index("band"), lax.axis_index("ga")
        self.low = self.band // 2 % 4
        self.line = self.low * nga + self.ga
        self.side = self.band // 8 * 2 + self.band % 2
        along = [8, 7, 9, 6, 10, 5, 11, 4, 12, 3, 13, 2, 14, 1, 15, 0]
        self.side_steps = [4, 5, 3, 2, 6, 7, 1]
        self.steps = [(z, x) for z in along for x in range(4) if z or x]

    def line_peer(self, step):
        z = lax.rem(self.ga // 4 * 4 + self.low + step[0], 16)
        return lax.rem(z, 4), z // 4 * 4 + lax.rem(lax.rem(self.ga, 4) + step[1], 4)

    def line_id(self, low, ga):
        return {"band": self.band // 8 * 8 + low * 2 + lax.rem(self.band, 2), "ga": ga}

    def side_peer(self, step):
        return lax.rem(self.side + step, 8)

    def side_id(self, side):
        return {"band": side // 2 * 8 + self.low * 2 + lax.rem(side, 2), "ga": self.ga}


def send(source, target, send_sem, recv_sem, device):
    pltpu.make_async_remote_copy(
        src_ref=source,
        dst_ref=target,
        send_sem=send_sem,
        recv_sem=recv_sem,
        device_id=device,
        device_id_type=MESH,
    ).start()


def kernel(
    nband, nga, spread, grid_scale,
    coeff_hbm, panel_hbm, pot_hbm, cols_hbm, tables_hbm, along_hbm, applied, inter,
    coeff, panel, pot, cols, cols_s, tables, along_z, first_v, first_s, window, place,
    send1, recv1, send2, recv2, sendp, linep, recvp, recv3,
    flat, grid, picked, stage, flatp, flat3, senda, recva, sendb, recvb,
    load, s1, r1, s2, r2, sp, rp, sq, rq, s3, r3, sa, ra, sb, rb,
):
    loads = [
        pltpu.make_async_copy(source, target, load.at[i])
        for i, (source, target) in enumerate(
            [
                (coeff_hbm, coeff),
                (along_hbm, along_z),
                (cols_hbm, cols),
                (cols_hbm, cols_s),
                (panel_hbm, panel),
                (pot_hbm, pot),
                (tables_hbm, tables),
            ]
        )
    ]
    for copy in loads:
        copy.start()
    me = Place(nband, nga)
    count_line, count_side = 4 * nga, nband // 4
    barrier = pltpu.get_barrier_semaphore()
    for step in me.steps:
        device = me.line_id(*me.line_peer(step))
        pl.semaphore_signal(barrier, inc=1, device_id=device, device_id_type=MESH)
    for step in me.side_steps:
        device = me.side_id(me.side_peer(step))
        pl.semaphore_signal(barrier, inc=1, device_id=device, device_id_type=MESH)

    def z_section(source, scale):
        own = lanes([source[part, band] for band in range(2) for part in range(2)])
        value = dot(along_z[...], own, 1, 1)
        if scale is not None:
            value = value * scale
        halves = [value[:, t * L : (t + 1) * L].reshape(count_line, 8, L) for t in range(2)]
        return jnp.concatenate(halves, axis=1).astype(BF16)

    loads[0].wait()
    loads[1].wait()
    send1[...] = z_section(coeff, spread)
    loads[4].wait()
    sendp[...] = z_section(panel, None)
    pl.semaphore_wait(barrier, count_line + count_side - 2)

    def to_slabs(source, target, send_sem, recv_sem):
        for step in me.steps:
            low, ga = me.line_peer(step)
            send(
                source.at[low * nga + ga], target.at[me.low, me.ga],
                send_sem, recv_sem.at[me.low], me.line_id(low, ga),
            )
        pltpu.make_async_copy(
            source.at[me.line], target.at[me.low, me.ga], recv_sem.at[me.low]
        ).start()

    to_slabs(send1, recv1, s1, r1)
    to_slabs(sendp, linep, sp, rp)

    loads[2].wait()
    loads[3].wait()
    col_x = lax.shift_right_logical(cols[...], 7)
    col_y = jnp.bitwise_and(cols[...], L - 1)
    blocks = col_x.shape[0]
    sub = iota((L, L), 0)
    lane = iota((L, L), 1)
    hot_x = lanes([one_hot(sub == col_x[t : t + 1, :]) for t in range(blocks)])
    hot_y = lanes([one_hot(sub == col_y[t : t + 1, :]) for t in range(blocks)])
    there = dot(hot_x, hot_y, 1, 1).astype(BF16)
    before = one_hot(sub < lane)
    ones = jnp.ones((L, L), BF16)
    rank = dot(there, before)
    below = dot(one_hot(lane < sub), there).astype(BF16)
    start = dot(below, ones).astype(jnp.int32)
    slot = start + rank.astype(jnp.int32)
    from_lane = jnp.bitwise_and(slot, L - 1)
    present = there.astype(F32) > 0.5
    first = lax.shift_right_logical(start, 7)
    lane_first = lane >= jnp.bitwise_and(start, L - 1)
    window[...] = jnp.where(lane_first, 1, 0)
    expand = rows([one_hot(first == lane), one_hot(first + 1 == lane)])[:, :blocks]
    where = dot(expand, lanes([col_y, col_x]).astype(F32).astype(BF16))
    sel_y = jnp.where(lane_first, block(where, 0, 0), block(where, 1, 0)).astype(jnp.int32)
    sel_x = jnp.where(lane_first, block(where, 0, 1), block(where, 1, 1)).astype(jnp.int32)
    place[...] = jnp.where(sel_x == sub, jnp.where(lane_first, 1, 2), 0)
    count = dot(ones, there, 1, 1).astype(BF16)
    start_row = dot(count, before)[:8].astype(jnp.int32)
    first_v[...] = jnp.minimum(lax.shift_right_logical(start_row, 7), blocks)
    to_scalars = pltpu.make_async_copy(first_v, first_s, load.at[7])
    to_scalars.start()
    flat[blocks:] = jnp.zeros((2, 8, L), F32)
    to_scalars.wait()

    def take(value, index):
        return jnp.take_along_axis(value, index, axis=1, mode="promise_in_bounds")

    def real_space(chunk):
        flat[:blocks] = recv1[chunk].astype(F32).reshape(blocks, 8, L)
        for x in range(L):
            at = first_s[0, x]
            grid[x * 8 : (x + 1) * 8, :] = jnp.where(
                window[x : x + 1, :] == 1, flat[at], flat[at + 1]
            )
        for pair in range(2):
            level = []
            for layer in range(2):
                planes = []
                for c in range(2):
                    run = grid[pl.ds(pair * 4 + c * 2 + layer, L, stride=8), :]
                    planes.append(jnp.where(present, take(run, from_lane), 0.0).astype(BF16))
                level.append(dot(lanes(planes), inverse).astype(BF16))
            turned = rows([lanes([one[:, c * L : (c + 1) * L] for one in level]) for c in range(2)])
            product = (dot(forward, turned) * rows([local, local])).astype(BF16)
            turned = rows([lanes([block(product, e, p) for e in range(2)]) for p in range(2)])
            level = dot(turned, forward).astype(BF16)
            turned = rows([lanes([block(level, p, c) for p in range(2)]) for c in range(2)])
            final = dot(inverse, turned) * grid_scale
            for p in range(2):
                for e in range(2):
                    picked[pl.ds(pair * 4 + e * 2 + p, L, stride=8), :] = take(
                        block(final, e, p), sel_y
                    )
        held = jnp.zeros((8, L), F32)
        for x in range(L):
            row = picked[x * 8 : (x + 1) * 8, :]
            part = place[x : x + 1, :]
            held = jnp.where(part == 1, row, held)
            stage[x] = held
            held = jnp.where(part == 2, row, held)
        for peer in range(nga):
            both = [
                stage[lax.shift_right_logical(cols_s[t, L - 1], 7)] for t in (2 * peer, 2 * peer + 1)
            ]
            send2[chunk, peer] = rows(both).astype(BF16)

    loads[5].wait()
    loads[6].wait()
    inverse, forward = tables[0], tables[1]
    local = lanes([pot[me.low * 2], pot[me.low * 2 + 1]])
    order_low = [2, 1, 3, 0]

    def send_picked(chunk):
        for step in me.side_steps:
            side = me.side_peer(step)
            send(
                send2.at[chunk, pl.ds(side * 2, 2)], recv3.at[me.side, chunk],
                s3, r3, me.side_id(side),
            )
        pltpu.make_async_copy(
            send2.at[chunk, pl.ds(me.side * 2, 2)], recv3.at[me.side, chunk], r3
        ).start()

    def send_back(step_low):
        chunk = lax.rem(me.low + step_low, 4)
        for step in (2, 1, 3, 0):
            for x in range(4):
                ga = lax.rem(me.ga // 4 + step, 4) * 4 + lax.rem(lax.rem(me.ga, 4) + x, 4)
                if step_low or step or x:
                    send(send2.at[chunk, ga], recv2.at[me.line], s2, r2, me.line_id(chunk, ga))
                else:
                    pltpu.make_async_copy(send2.at[chunk, ga], recv2.at[me.line], r2).start()

    for step_low in order_low:
        chunk = lax.rem(me.low + step_low, 4)
        wait_all(recv1.at[chunk], r1.at[chunk])
        real_space(chunk)
        send_picked(chunk)

    for low in range(4):
        wait_all(linep.at[low], rp.at[low])
    for step in me.side_steps:
        side = me.side_peer(step)
        send(linep.at[:, pl.ds(side * 2, 2)], recvp.at[me.side], sq, rq, me.side_id(side))
    pltpu.make_async_copy(linep.at[:, pl.ds(me.side * 2, 2)], recvp.at[me.side], rq).start()
    for step_low in order_low:
        send_back(step_low)

    def gram_rows(wide, part):
        taken = []
        for share in range(2):
            for t in range(2):
                for layer in range(2):
                    at = [share * 16 + t * 8 + b * 4 + part * 2 + layer for b in range(2)]
                    taken.append(rows([wide[pl.ds(one, nband, stride=32), :] for one in at]))
        return lanes(taken).astype(BF16)

    wait_all(recv3, r3)
    flat3[...] = recv3[...].astype(F32).reshape(nband * 32, L)
    right = [gram_rows(flat3, part) for part in range(2)]
    right = rows([lanes(right), lanes([right[1], -right[0]])])
    wait_all(recvp, rq)
    flatp[...] = recvp[...].astype(F32).reshape(nband * 32, L)
    left = lanes([gram_rows(flatp, part) for part in range(2)])
    value = dot(left, right, 1, 1) * spread
    for side in range(8):
        for b in range(2):
            senda[side, b * 4 : b * 4 + 4] = value[b * nband + side * 4 : b * nband + side * 4 + 4]
    for step in me.side_steps:
        side = me.side_peer(step)
        send(senda.at[side], recva.at[me.side], sa, ra, me.side_id(side))
    recva[me.side] = senda[me.side]
    wait_all(recva.at[pl.ds(0, count_side - 1)], ra)
    summed = jnp.sum(recva[...], axis=0)
    column = iota((8, L), 1)
    inner = lax.rem(column, L // 2)
    for half in range(2):
        index = inner // 2 * 4 + lax.rem(inner, 2) + half * 2
        both = take(summed, index)
        for low in range(4):
            pair = [both[b * 4 + low : b * 4 + low + 1] for b in range(2)]
            sendb[low, half] = jnp.where(column[:1] < L // 2, pair[0], pair[1])
    for step in me.steps:
        low, ga = me.line_peer(step)
        send(sendb.at[low, lax.rem(ga, 4) // 2], recvb.at[me.line], sb, rb, me.line_id(low, ga))
    recvb[me.line] = sendb[me.low, lax.rem(me.ga, 4) // 2]

    wait_all(recv2, r2)
    got = recv2[...].astype(F32)
    own = lanes([got[:, t * 8 : t * 8 + 8].reshape(8 * count_line, L) for t in range(2)])
    result = dot(own.astype(BF16), along_z[...], 0, 0).astype(BF16)
    for band in range(2):
        for e in range(2):
            at = (band * 2 + e) * L
            applied[e, band] = result[:, at : at + L]

    wait_all(recvb.at[pl.ds(0, count_line - 1)], rb)
    total = jnp.sum(recvb[...], axis=0)
    total = rows([total, jnp.zeros((7, L), F32)])
    width = inter.shape[2]
    base = me.ga // 4 * 4 + lax.rem(me.ga, 2)
    for e in range(2):
        for b in range(2):
            index = b * 64 + e * 32 + base + lax.rem(column, 2) * 16 + lax.rem(column // 2, 2) * 2
            inter[e, b : b + 1] = take(total, index)[:1, :width]

    wait_all(send1.at[pl.ds(0, count_line - 1)], s1)
    wait_all(send1.at[pl.ds(0, count_line - 1)], sp)
    wait_all(send1.at[pl.ds(0, count_line - 1)], s2)
    wait_all(recv3.at[pl.ds(0, count_side - 1)], s3)
    wait_all(recvp.at[pl.ds(0, count_side - 1)], sq)
    wait_all(senda.at[pl.ds(0, count_side - 1)], sa)
    wait_all(recvb.at[pl.ds(0, count_line - 1)], sb)


def solution(mesh):
    nband, nga = mesh.shape["band"], mesh.shape["ga"]

    def per_device(coefficients, panel, potential, stick_columns):
        sticks = stick_columns.shape[0]
        depth = coefficients.shape[3]
        blocks = sticks // L
        line, side = 4 * nga, nband // 4
        spread = 1.0 / math.sqrt(sticks * depth)
        grid_scale = 1.0 / math.sqrt(L * L * depth)
        inverse = section_table()
        tables = np.stack([inverse, inverse.T])
        split = inverse.T.reshape(2, nga, 4, 2, 2 * L).transpose(2, 1, 0, 3, 4)
        along = np.zeros((4, nga, 2, 2, 2, 2, 2 * L))
        for band in range(2):
            along[:, :, band, :, :, band] = split
        along = along.reshape(8 * line, 4 * L)
        vmem = pl.BlockSpec(memory_space=pltpu.VMEM)
        hbm = pl.BlockSpec(memory_space=pl.ANY)
        dma = pltpu.SemaphoreType.DMA
        line_tiles = pltpu.VMEM((line, 16, L), BF16)
        slab_tiles = pltpu.VMEM((4, nga, 16, L), BF16)
        side_tiles = pltpu.VMEM((side, 4, 2, 16, L), BF16)
        applied, intersection = pl.pallas_call(
            functools.partial(kernel, nband, nga, spread, grid_scale),
            out_shape=(
                jax.ShapeDtypeStruct(coefficients.shape, BF16),
                jax.ShapeDtypeStruct((2, 2, 2 * nband // nga), F32),
            ),
            in_specs=[hbm] * 6,
            out_specs=(vmem, vmem),
            scratch_shapes=[
                pltpu.VMEM(coefficients.shape, BF16),
                pltpu.VMEM(panel.shape, BF16),
                pltpu.VMEM(potential.shape, F32),
                pltpu.VMEM((blocks, L), jnp.int32),
                pltpu.SMEM((blocks, L), jnp.int32),
                pltpu.VMEM(tables.shape, BF16),
                pltpu.VMEM(along.shape, BF16),
                pltpu.VMEM((8, L), jnp.int32),
                pltpu.SMEM((8, L), jnp.int32),
                pltpu.VMEM((L, L), jnp.int32),
                pltpu.VMEM((L, L), jnp.int32),
                line_tiles, slab_tiles, slab_tiles, line_tiles,
                line_tiles, slab_tiles, side_tiles, side_tiles,
                pltpu.VMEM((blocks + 2, 8, L), F32),
                pltpu.VMEM((L * 8, L), F32),
                pltpu.VMEM((L * 8, L), F32),
                pltpu.VMEM((L, 8, L), F32),
                pltpu.VMEM((nband * 32, L), F32),
                pltpu.VMEM((nband * 32, L), F32),
                pltpu.VMEM((side, 8, L), F32),
                pltpu.VMEM((side, 8, L), F32),
                pltpu.VMEM((4, 2, 1, L), F32),
                pltpu.VMEM((line, 1, L), F32),
                dma((8,)), dma, dma((4,)), dma, dma, dma, dma((4,)), dma, dma,
                dma, dma, dma, dma, dma, dma,
            ],
            compiler_params=pltpu.CompilerParams(
                collective_id=0, has_side_effects=True, vmem_limit_bytes=48 * 2**20
            ),
        )(
            *[
                pltpu.with_memory_space_constraint(one, pltpu.HBM)
                for one in (
                    coefficients,
                    panel,
                    potential,
                    stick_columns.reshape(blocks, L),
                    jnp.asarray(tables.astype(ml_dtypes.bfloat16)),
                    jnp.asarray(along.astype(ml_dtypes.bfloat16)),
                )
            ]
        )
        return applied, intersection

    in_specs = (P(None, "band", "ga", None), P(None, "band", "ga", None), P("ga", None, None), P())
    out_specs = (P(None, "band", "ga", None), P(None, "band", "ga"))
    return jax.shard_map(
        per_device, mesh=mesh, in_specs=in_specs, out_specs=out_specs, check_vma=False
    )
```
